32 devices in a mesh: groups: 2 (over y), bricks: 4 (over z), sub: 4 (over x, core).
Axes of the slice: x: 2, y: 2, z: 4, core: 2. Of those that a mesh axis runs over, the one named last changes fastest.
Arguments:
- features: bfloat16 [32768, 256], P(('groups', 'bricks', 'sub')), parts along dimension 0, may hold values from -6 to 6
- active: int32 [64], P(('groups', 'bricks', 'sub')), parts along dimension 0, may hold values 0 or 1
- weight: bfloat16 [27, 256, 128], replicated, may hold values from -0.078125 to 0.078125
- cotangent: bfloat16 [32768, 128], P(('groups', 'bricks', 'sub')), parts along dimension 0, may hold values from -6 to 6
Outputs:
- conv_out: bfloat16 [32768, 128], P(('groups', 'bricks', 'sub')), parts along dimension 0
- grad_features: bfloat16 [32768, 256], P(('groups', 'bricks', 'sub')), parts along dimension 0
- grad_weight: bfloat16 [54, 256, 128], P('groups'), parts along dimension 0
The draws below stay inside these ranges and needn't reach their ends.
There are 2 independent parts, one for each index of `groups`. The reference program is written for one: setup_inputs(seed, part) draws one part's arguments, and reference() takes and returns one part's arrays. A program takes and returns all parts, laid end to end along the dimension named above; an argument that names none is the same for every part. Nothing has to cross between parts.
All inputs are finite; a program needn't handle non-finite values. No bound on the sum of `active` on one device may be relied on, other than what follows from the above.
Results may differ from the reference program's by a relative error of at most 0.003.
Values may be sent and summed in bfloat16 or wider, within the bound.
A program may use at most 64 MiB of HBM per device.

```python
import jax
import jax.numpy as jnp
from jax import lax

CIN = 256
COUT = 128
EDGE = 8
BR_DEV = 2
NB = 32
ROWS = 16384
N_BRICKS = 4
N_SUB = 4


def touch_ends(values, key, smallest, top_value):
    longest = values.shape.index(max(values.shape))
    spots = []
    for shift in (0, 1):
        where = [jax.random.randint(jax.random.fold_in(key, axis), (), 0, length) for axis, length in enumerate(values.shape)]
        where[longest] = (where[longest] + shift) % values.shape[longest]
        spots.append(tuple(where))
    return values.at[spots[0]].set(smallest).at[spots[1]].set(top_value)


def level_of(stream_key, shape, split, smallest, largest):
    loudness = 1.0
    for axis_at, parts in split:
        steps = jax.random.uniform(jax.random.fold_in(jax.random.fold_in(stream_key, 6), axis_at), (parts,), jnp.float32, smallest / len(split), largest / len(split))
        loudness = loudness * jnp.repeat(jnp.exp(steps), shape[axis_at] // parts).reshape((-1,) + (1,) * (len(shape) - 1 - axis_at))
    return loudness


def normal_values(stream_key, shape, width, reach, split=(), dtype=jnp.bfloat16):
    array = jax.random.normal(stream_key, shape, jnp.float32) * width
    if len(split) > 0:
        array = level_of(stream_key, shape, split, -0.22, 0.18) * array
    return jnp.clip(array, min=-reach, max=reach).astype(dtype)


def setup_inputs(seed: int = 0, part: int = 0) -> dict:
    streams_of = jax.random.split(jax.random.key(seed), 5)
    part_splits = jax.random.split(jax.random.fold_in(streams_of[4], part), 5)
    features = normal_values(part_splits[0], (ROWS, CIN), 1.0, 6.0, ((0, 16),))
    active = touch_ends((jax.random.randint(part_splits[1], (NB,), 0, 5) < 3).astype(jnp.int32), jax.random.fold_in(part_splits[1], 1), 0, 1)
    weight = normal_values(streams_of[2], (27, CIN, COUT), (27 * CIN) ** -0.5, 0.078125)
    cotangent = normal_values(part_splits[3], (ROWS, COUT), 1.0, 6.0, ((0, 16),))
    return dict(features=features, active=active, weight=weight, cotangent=cotangent)


def to_dense(field_rows):
    channel_count = field_rows.shape[1]
    bricks = field_rows.reshape(N_BRICKS, N_SUB, BR_DEV, EDGE, EDGE, EDGE, channel_count)
    bricks = bricks.transpose(0, 3, 1, 4, 2, 5, 6)
    return bricks.reshape(N_BRICKS * EDGE, N_SUB * EDGE, BR_DEV * EDGE, channel_count)

def from_dense(dense_grid):
    channel_count = dense_grid.shape[3]
    bricks = dense_grid.reshape(N_BRICKS, EDGE, N_SUB, EDGE, BR_DEV, EDGE, channel_count)
    bricks = bricks.transpose(0, 2, 4, 1, 3, 5, 6)
    return bricks.reshape(-1, channel_count)

def reference(features, active, weight, cotangent):
    live_rows = jnp.repeat(active.astype(jnp.float32), EDGE ** 3)[:, None]
    masked_features = features.astype(jnp.float32) * live_rows
    masked_grads = cotangent.astype(jnp.float32) * live_rows
    kernel = weight.astype(jnp.float32).reshape(3, 3, 3, CIN, COUT)

    def convolve(field_rows, taps):
        result = lax.conv_general_dilated(to_dense(field_rows)[None], taps, (1, 1, 1), 'SAME', dimension_numbers=('NDHWC', 'DHWIO', 'NDHWC'), precision=lax.Precision.HIGHEST)
        return from_dense(result[0])
    response, pullback = jax.vjp(convolve, masked_features, kernel)
    conv_out = (response * live_rows).astype(jnp.bfloat16)
    grad_field, grad_taps = pullback(masked_grads)
    grad_features = (grad_field * live_rows).astype(jnp.bfloat16)
    grad_weight = (grad_taps.reshape(27, CIN, COUT) * (1.0 / ROWS ** 0.5)).astype(jnp.bfloat16)
    return (conv_out, grad_features, grad_weight)
```

```python
import functools
import math

import jax
import jax.numpy as jnp
from jax import lax
from jax.experimental import pallas as pl
from jax.experimental.pallas import tpu as pltpu
from jax.sharding import PartitionSpec as P

EDGE = 8
MESH = pl.DeviceIdType.MESH
X_TYPE = jnp.bfloat16
Z_TYPE = jnp.float32
SIDES = [(i, j) for i in (-1, 0, 1) for j in (-1, 0, 1) if (i, j) != (0, 0)]


def own_side(step):
    return pl.ds(1, EDGE) if step == 0 else pl.ds(EDGE if step > 0 else 1, 1)


def far_side(step):
    return pl.ds(1, EDGE) if step == 0 else pl.ds(0 if step > 0 else EDGE + 1, 1)


def kernel(
    n, m, fused, grad_scale,
    feat_ref, act_ref, weight_hbm, cot_ref,
    conv_ref, gfeat_ref, gw_hbm,
    fp, gp, gcat, ft, w_ref, conv_acc, back_acc, ks, r1, s2, r2, kept, s3, r3, out,
    halo_send, halo_recv, send, recv, local_sem,
):
    g, b, s = lax.axis_index("groups"), lax.axis_index("bricks"), lax.axis_index("sub")
    bricks_dev = act_ref.shape[0]
    depth = bricks_dev * EDGE
    brick_rows = EDGE**3
    cin, cout = feat_ref.shape[1], cot_ref.shape[1]
    plane = EDGE * depth
    rows = EDGE * plane

    def inside(db, ds):
        return (b + db >= 0) & (b + db < n) & (s + ds >= 0) & (s + ds < m)

    w_copy = pltpu.make_async_copy(weight_hbm, w_ref, local_sem.at[0])
    w_copy.start()
    for field in (fp, gp):
        edge_row = jnp.zeros((EDGE + 2, depth, field.shape[3]), jnp.bfloat16)
        edge_col = jnp.zeros((EDGE, 1, depth, field.shape[3]), jnp.bfloat16)
        field[0] = edge_row
        field[EDGE + 1] = edge_row
        field[1 : EDGE + 1, 0:1] = edge_col
        field[1 : EDGE + 1, EDGE + 1 : EDGE + 2] = edge_col

    barrier = pltpu.get_barrier_semaphore()
    if fused:
        for i in range(n):
            for j in range(m):
                if (i, j) != (0, 0):
                    pl.semaphore_signal(
                        barrier, inc=1, device_id=(g, lax.rem(b + i, n), lax.rem(s + j, m)), device_id_type=MESH
                    )
    else:
        for db, ds in SIDES:
            @pl.when(inside(db, ds))
            def _():
                pl.semaphore_signal(barrier, inc=1, device_id=(g, b + db, s + ds), device_id_type=MESH)

    def place(source, target):
        def one(i, _):
            pieces = []
            for l in range(bricks_dev):
                start = pl.multiple_of(l * brick_rows + i * EDGE * EDGE, EDGE * EDGE)
                piece = source[pl.ds(start, EDGE * EDGE), :].astype(jnp.float32)
                piece = piece * act_ref[l].astype(jnp.float32)
                pieces.append(piece.reshape(EDGE, 1, EDGE, source.shape[1]))
            both = jnp.concatenate(pieces, axis=1).reshape(EDGE, depth, source.shape[1])
            target[i + 1, 1 : EDGE + 1] = both.astype(jnp.bfloat16)
            return 0

        lax.fori_loop(0, EDGE, one, 0)

    place(cot_ref, gp)
    place(feat_ref, fp)

    if fused:
        pl.semaphore_wait(barrier, n * m - 1)
    else:
        for db, ds in SIDES:
            @pl.when(inside(db, ds))
            def _():
                pl.semaphore_wait(barrier, 1)

    def halo(field_at, side):
        field = (gp, fp)[field_at]
        db, ds = SIDES[side]
        return pltpu.make_async_remote_copy(
            src_ref=field.at[own_side(db), own_side(ds)],
            dst_ref=field.at[far_side(db), far_side(ds)],
            send_sem=halo_send.at[field_at, side],
            recv_sem=halo_recv.at[field_at, side],
            device_id=(g, b + db, s + ds),
            device_id_type=MESH,
        )

    for field_at in range(2):
        for side, (db, ds) in enumerate(SIDES):
            @pl.when(inside(db, ds))
            def _():
                halo(field_at, side).start()

    def wait_halo(field_at):
        for side, (db, ds) in enumerate(SIDES):
            @pl.when(inside(-db, -ds))
            def _():
                halo(field_at, side).wait_recv()

    def turn(i, _):
        start = pl.multiple_of(i * plane, plane)
        piece = fp[i + 1, 1 : EDGE + 1].reshape(plane, cin)
        ft[:, pl.ds(start, plane)] = piece.astype(jnp.float32).T.astype(jnp.bfloat16)
        return 0

    lax.fori_loop(0, EDGE, turn, 0)
    wait_halo(0)

    def widen(i, _):
        count = (EDGE + 2) * depth
        middle = gp[i].astype(jnp.float32).reshape(count, cout)
        at = lax.rem(lax.broadcasted_iota(jnp.int32, (count, cout), 0), depth)
        later = jnp.where(at == depth - 1, 0.0, pltpu.roll(middle, count - 1, 0))
        earlier = jnp.where(at == 0, 0.0, pltpu.roll(middle, 1, 0))
        wide = jnp.concatenate([later, middle, earlier], axis=1)
        gcat[i] = wide.astype(jnp.bfloat16).reshape(EDGE + 2, depth, 3 * cout)
        return 0

    lax.fori_loop(0, EDGE + 2, widen, 0)

    def grads_at(p):
        first, mid = p // 3, p % 3
        return gcat[2 - first : 2 - first + EDGE, 2 - mid : 2 - mid + EDGE].reshape(rows, 3 * cout)

    def weights_at(p):
        return jnp.concatenate([w_ref[3 * p], w_ref[3 * p + 1], w_ref[3 * p + 2]], axis=1)

    def tap_sums(p):
        sums = jnp.dot(ft[...], grads_at(p), preferred_element_type=jnp.float32)
        for last in range(3):
            ks[p, last * cin : (last + 1) * cin] = sums[:, last * cout : (last + 1) * cout]

    def forward(p):
        first, mid = p // 3, p % 3
        field = fp[first : first + EDGE, mid : mid + EDGE].reshape(rows, cin)
        term = jnp.dot(field, weights_at(p), preferred_element_type=jnp.float32)
        if p == 0:
            conv_acc[...] = term
        else:
            conv_acc[...] += term

    def backward(p):
        term = lax.dot_general(
            grads_at(p), weights_at(p), (((1,), (1,)), ((), ())), preferred_element_type=jnp.float32
        )
        if p == 0:
            back_acc[...] = term
        else:
            back_acc[...] += term

    def write_rows(i, value, target):
        width = target.shape[1]
        parts = value.reshape(EDGE, bricks_dev, EDGE, width)
        for l in range(bricks_dev):
            start = pl.multiple_of(l * brick_rows + i * EDGE * EDGE, EDGE * EDGE)
            piece = parts[:, l].reshape(EDGE * EDGE, width) * act_ref[l].astype(jnp.float32)
            target[pl.ds(start, EDGE * EDGE), :] = piece.astype(jnp.bfloat16)

    def write_forward():
        def one(i, _):
            start = pl.multiple_of(i * plane, plane)
            at = lax.rem(lax.broadcasted_iota(jnp.int32, (plane, cout), 0), depth)
            before = conv_acc[pl.ds(start, plane), 0:cout]
            middle = conv_acc[pl.ds(start, plane), cout : 2 * cout]
            after = conv_acc[pl.ds(start, plane), 2 * cout : 3 * cout]
            value = middle + jnp.where(at == 0, 0.0, pltpu.roll(before, 1, 0))
            value = value + jnp.where(at == depth - 1, 0.0, pltpu.roll(after, plane - 1, 0))
            write_rows(i, value, conv_ref)
            return 0

        lax.fori_loop(0, EDGE, one, 0)

    def write_backward():
        def one(i, _):
            start = pl.multiple_of(i * plane, plane)
            write_rows(i, back_acc[pl.ds(start, plane), :], gfeat_ref)
            return 0

        lax.fori_loop(0, EDGE, one, 0)

    jobs = [functools.partial(backward, p) for p in range(9)] + [write_backward]
    jobs += [functools.partial(forward, p) for p in range(9)] + [write_forward]
    jobs[0:0] = [w_copy.wait]
    jobs[11:11] = [lambda: wait_halo(1)]

    if not fused:
        for p in range(9):
            tap_sums(p)
        for job in jobs:
            job()
        local = pltpu.make_async_copy(ks, gw_hbm, local_sem.at[1])
        local.start()
        local.wait()
    else:
        core = lax.rem(s, 2)
        x = s // 2
        group_rows = 3 * cin
        half, quarter = group_rows // 2, group_rows // 4
        chunk = quarter // n
        twin = (g, b, s + 1 - 2 * core)
        across = (g, b, lax.rem(s + 2, m))

        def aligned(value):
            return pl.multiple_of(value, 16)

        def along(step):
            return (g, lax.rem(b + step, n), s)

        def remote(p, slot, src, dst, device):
            return pltpu.make_async_remote_copy(
                src_ref=src, dst_ref=dst, send_sem=send.at[p, slot], recv_sem=recv.at[p, slot],
                device_id=device, device_id_type=MESH,
            )

        mine = aligned(core * half)
        mine_x = aligned(core * half + x * quarter)
        mine_z = aligned(core * half + x * quarter + b * chunk)

        def pair_copy(p):
            return remote(p, 0, ks.at[p, pl.ds(aligned((1 - core) * half), half)], r1.at[p], twin)

        def across_copy(p):
            return remote(p, 1, s2.at[p], r2.at[p], across)

        def along_copy(p, step):
            to = lax.rem(b + step, n)
            return remote(p, 1 + step, s3.at[p, to], r3.at[p, step - 1], along(step))

        def along_back(p, step):
            part = out.at[p, pl.ds(mine_z, chunk)]
            return remote(p, n + step, part, part, along(step))

        def across_back(p):
            part = out.at[p, pl.ds(mine_x, quarter)]
            return remote(p, 2 * n, part, part, across)

        def pair_back(p):
            part = out.at[p, pl.ds(mine, half)]
            return remote(p, 2 * n + 1, part, part, twin)

        def write_out(p):
            return pltpu.make_async_copy(out.at[p], gw_hbm.at[p], local_sem.at[1 + p])

        def stage0(p):
            tap_sums(p)
            pair_copy(p).start()

        def stage1(p):
            pair_copy(p).wait_recv()
            theirs = aligned((1 - x) * quarter)
            total = ks[p, pl.ds(aligned(core * half + (1 - x) * quarter), quarter)] + r1[p, pl.ds(theirs, quarter)]
            s2[p] = total.astype(X_TYPE)
            across_copy(p).start()
            kept[p] = ks[p, pl.ds(mine_x, quarter)] + r1[p, pl.ds(aligned(x * quarter), quarter)]

        def stage2(p):
            across_copy(p).wait_recv()
            total = kept[p] + r2[p].astype(jnp.float32)
            kept[p] = total
            s3[p] = total.astype(Z_TYPE).reshape(n, chunk, cout)
            for step in range(1, n):
                along_copy(p, step).start()

        def stage3(p):
            total = kept[p, pl.ds(aligned(b * chunk), chunk)]
            for step in range(1, n):
                along_copy(p, step).wait_recv()
                total = total + r3[p, step - 1].astype(jnp.float32)
            out[p, pl.ds(mine_z, chunk)] = (total * grad_scale).astype(jnp.bfloat16)
            for step in range(1, n):
                along_back(p, step).start()

        def stage4(p):
            for step in range(1, n):
                along_back(p, step).wait_recv()
            across_back(p).start()

        def stage5(p):
            across_back(p).wait_recv()
            pair_back(p).start()

        def stage6(p):
            pair_back(p).wait_recv()
            write_out(p).start()

        stages = [stage0, stage1, stage2, stage3, stage4, stage5, stage6]
        for t in range(9 + 6):
            for k in reversed(range(7)):
                if 0 <= t - k < 9:
                    stages[k](t - k)
            if t >= 1:
                for job in jobs[:2]:
                    job()
                jobs = jobs[2:]
        for job in jobs:
            job()
        for p in range(9):
            pair_copy(p).wait_send()
            across_copy(p).wait_send()
            for step in range(1, n):
                along_copy(p, step).wait_send()
                along_back(p, step).wait_send()
            across_back(p).wait_send()
            pair_back(p).wait_send()
            write_out(p).wait()

    for field_at in range(2):
        for side, (db, ds) in enumerate(SIDES):
            @pl.when(inside(db, ds))
            def _():
                halo(field_at, side).wait_send()


def shards(features, active, weight, cotangent):
    n, m = lax.axis_size("bricks"), lax.axis_size("sub")
    bricks_dev = active.shape[0]
    cin, cout = features.shape[1], weight.shape[2]
    rows = features.shape[0]
    depth = bricks_dev * EDGE
    group_rows = 3 * cin
    fused = m == 4 and group_rows % (4 * n * 16) == 0
    quarter = group_rows // 4
    chunk = quarter // n if fused else 16
    slots = 2 * n + 2 if fused else 1
    groups = 9 if fused else 1
    grad_scale = 1.0 / math.sqrt(n * m * rows)
    bf16, f32 = jnp.bfloat16, jnp.float32
    vmem = pl.BlockSpec(memory_space=pltpu.VMEM)
    scratch = [
        pltpu.VMEM((EDGE + 2, EDGE + 2, depth, cin), bf16),
        pltpu.VMEM((EDGE + 2, EDGE + 2, depth, cout), bf16),
        pltpu.VMEM((EDGE + 2, EDGE + 2, depth, 3 * cout), bf16),
        pltpu.VMEM((cin, rows), bf16),
        pltpu.VMEM(weight.shape, bf16),
        pltpu.VMEM((rows, 3 * cout), f32),
        pltpu.VMEM((rows, cin), f32),
        pltpu.VMEM((9, group_rows, cout), f32),
        pltpu.VMEM((groups, group_rows // 2, cout), f32),
        pltpu.VMEM((groups, quarter, cout), X_TYPE),
        pltpu.VMEM((groups, quarter, cout), X_TYPE),
        pltpu.VMEM((groups, quarter, cout), f32),
        pltpu.VMEM((groups, n, chunk, cout), Z_TYPE),
        pltpu.VMEM((groups, n - 1, chunk, cout), Z_TYPE),
        pltpu.VMEM((groups, group_rows, cout), bf16),
        pltpu.SemaphoreType.DMA((2, 8)),
        pltpu.SemaphoreType.DMA((2, 8)),
        pltpu.SemaphoreType.DMA((groups, slots)),
        pltpu.SemaphoreType.DMA((groups, slots)),
        pltpu.SemaphoreType.DMA((10,)),
    ]
    conv_out, grad_features, grad_weight = pl.pallas_call(
        functools.partial(kernel, n, m, fused, grad_scale),
        out_shape=(
            jax.ShapeDtypeStruct((rows, cout), bf16),
            jax.ShapeDtypeStruct((rows, cin), bf16),
            jax.ShapeDtypeStruct((9, group_rows, cout), bf16 if fused else f32),
        ),
        in_specs=[vmem, pl.BlockSpec(memory_space=pltpu.SMEM), pl.BlockSpec(memory_space=pl.ANY), vmem],
        out_specs=(vmem, vmem, pl.BlockSpec(memory_space=pl.ANY)),
        scratch_shapes=scratch,
        compiler_params=pltpu.CompilerParams(
            collective_id=0, has_side_effects=True, vmem_limit_bytes=48 * 1024 * 1024
        ),
    )(features, active, weight, cotangent)
    grad_weight = grad_weight.reshape(27, cin, cout)
    if not fused:
        grad_weight = (lax.psum(grad_weight, ("bricks", "sub")) * grad_scale).astype(bf16)
    return (conv_out, grad_features, grad_weight)


def solution(mesh):
    in_specs = (
        P(("groups", "bricks", "sub"), None),
        P(("groups", "bricks", "sub")),
        P(),
        P(("groups", "bricks", "sub"), None),
    )
    out_specs = (
        P(("groups", "bricks", "sub"), None),
        P(("groups", "bricks", "sub"), None),
        P("groups", None, None),
    )
    return jax.shard_map(shards, mesh=mesh, in_specs=in_specs, out_specs=out_specs, check_vma=False)
```

```python
import functools
import math

import jax
import jax.numpy as jnp
from jax import lax
from jax.experimental import pallas as pl
from jax.experimental.pallas import tpu as pltpu
from jax.sharding import PartitionSpec as P

EDGE = 8
MESH = pl.DeviceIdType.MESH
LEVELS = 4
WIRE = (jnp.float32, jnp.bfloat16, jnp.float32, jnp.float32)
STARTS = (0, 2, 4, 6, 8, 10, 12, 14, 16)
PER_STEP = 1
VMEM_LIMIT = 60 * 1024 * 1024
SIDES = [(i, j) for i in (-1, 0, 1) for j in (-1, 0, 1) if (i, j) != (0, 0)]


def own_side(step):
    return pl.ds(1, EDGE) if step == 0 else pl.ds(EDGE if step > 0 else 1, 1)


def far_side(step):
    return pl.ds(1, EDGE) if step == 0 else pl.ds(0 if step > 0 else EDGE + 1, 1)


def kernel(
    n, m, fused, grad_scale,
    feat_hbm, act_ref, weight_hbm, cot_hbm,
    conv_ref, gfeat_ref, gw_hbm,
    feat_ref, cot_ref, fp, gp, gcat, ft, w_ref, conv_acc, back_acc, ks, out,
    got, sent, kept, halo_send, halo_recv, send, recv, local_sem,
):
    g, b, s = lax.axis_index("groups"), lax.axis_index("bricks"), lax.axis_index("sub")
    bricks_dev = act_ref.shape[0]
    depth = bricks_dev * EDGE
    brick_rows = EDGE**3
    cin, cout = feat_ref.shape[1], cot_ref.shape[1]
    plane = EDGE * depth
    rows = EDGE * plane

    def inside(db, ds):
        return (b + db >= 0) & (b + db < n) & (s + ds >= 0) & (s + ds < m)

    w_copy = pltpu.make_async_copy(weight_hbm, w_ref, local_sem.at[0])
    feat_copy = pltpu.make_async_copy(feat_hbm, feat_ref, local_sem.at[10])
    cot_copy = pltpu.make_async_copy(cot_hbm, cot_ref, local_sem.at[11])
    cot_copy.start()
    feat_copy.start()
    w_copy.start()
    for field in (fp, gp):
        edge_row = jnp.zeros((EDGE + 2, depth, field.shape[3]), jnp.bfloat16)
        edge_col = jnp.zeros((EDGE, 1, depth, field.shape[3]), jnp.bfloat16)
        field[0] = edge_row
        field[EDGE + 1] = edge_row
        field[1 : EDGE + 1, 0:1] = edge_col
        field[1 : EDGE + 1, EDGE + 1 : EDGE + 2] = edge_col

    barrier = pltpu.get_barrier_semaphore()
    if fused:
        for i in range(n):
            for j in range(m):
                if (i, j) != (0, 0):
                    pl.semaphore_signal(
                        barrier, inc=1, device_id=(g, lax.rem(b + i, n), lax.rem(s + j, m)), device_id_type=MESH
                    )
    else:
        for db, ds in SIDES:
            @pl.when(inside(db, ds))
            def _():
                pl.semaphore_signal(barrier, inc=1, device_id=(g, b + db, s + ds), device_id_type=MESH)

    def place(source, target):
        def one(i, _):
            pieces = []
            for l in range(bricks_dev):
                start = pl.multiple_of(l * brick_rows + i * EDGE * EDGE, EDGE * EDGE)
                piece = source[pl.ds(start, EDGE * EDGE), :].astype(jnp.float32)
                piece = piece * act_ref[l].astype(jnp.float32)
                pieces.append(piece.reshape(EDGE, 1, EDGE, source.shape[1]))
            both = jnp.concatenate(pieces, axis=1).reshape(EDGE, depth, source.shape[1])
            target[i + 1, 1 : EDGE + 1] = both.astype(jnp.bfloat16)
            return 0

        lax.fori_loop(0, EDGE, one, 0)

    cot_copy.wait()
    place(cot_ref, gp)

    if fused:
        pl.semaphore_wait(barrier, n * m - 1)
    else:
        for db, ds in SIDES:
            @pl.when(inside(db, ds))
            def _():
                pl.semaphore_wait(barrier, 1)

    def halo(field_at, side):
        field = (gp, fp)[field_at]
        db, ds = SIDES[side]
        return pltpu.make_async_remote_copy(
            src_ref=field.at[own_side(db), own_side(ds)],
            dst_ref=field.at[far_side(db), far_side(ds)],
            send_sem=halo_send.at[field_at, side],
            recv_sem=halo_recv.at[field_at, side],
            device_id=(g, b + db, s + ds),
            device_id_type=MESH,
        )

    def start_halo(field_at):
        for side, (db, ds) in enumerate(SIDES):
            @pl.when(inside(db, ds))
            def _():
                halo(field_at, side).start()

    start_halo(0)
    feat_copy.wait()
    place(feat_ref, fp)
    start_halo(1)

    def wait_halo(field_at):
        for side, (db, ds) in enumerate(SIDES):
            @pl.when(inside(-db, -ds))
            def _():
                halo(field_at, side).wait_recv()

    def turn(i, _):
        start = pl.multiple_of(i * plane, plane)
        piece = fp[i + 1, 1 : EDGE + 1].reshape(plane, cin)
        ft[:, pl.ds(start, plane)] = piece.astype(jnp.float32).T.astype(jnp.bfloat16)
        return 0

    lax.fori_loop(0, EDGE, turn, 0)
    wait_halo(0)

    def widen(i, _):
        count = (EDGE + 2) * depth
        middle = gp[i].astype(jnp.float32).reshape(count, cout)
        at = lax.broadcasted_iota(jnp.int32, (EDGE + 2, depth, cout), 1).reshape(count, cout)
        later = jnp.where(at == depth - 1, 0.0, pltpu.roll(middle, count - 1, 0))
        earlier = jnp.where(at == 0, 0.0, pltpu.roll(middle, 1, 0))
        wide = jnp.concatenate([later, middle, earlier], axis=1)
        gcat[i] = wide.astype(jnp.bfloat16).reshape(EDGE + 2, depth, 3 * cout)
        return 0

    lax.fori_loop(0, EDGE + 2, widen, 0)

    def grads_at(p):
        first, mid = p // 3, p % 3
        return gcat[2 - first : 2 - first + EDGE, 2 - mid : 2 - mid + EDGE].reshape(rows, 3 * cout)

    def weights_at(p):
        return jnp.concatenate([w_ref[3 * p], w_ref[3 * p + 1], w_ref[3 * p + 2]], axis=1)

    def tap_sums(p):
        sums = jnp.dot(ft[...], grads_at(p), preferred_element_type=jnp.float32)
        for last in range(3):
            ks[p, last * cin : (last + 1) * cin] = sums[:, last * cout : (last + 1) * cout]

    def forward(p):
        first, mid = p // 3, p % 3
        field = fp[first : first + EDGE, mid : mid + EDGE].reshape(rows, cin)
        term = jnp.dot(field, weights_at(p), preferred_element_type=jnp.float32)
        if p == 0:
            conv_acc[...] = term
        else:
            conv_acc[...] += term

    def backward(p):
        term = lax.dot_general(
            grads_at(p), weights_at(p), (((1,), (1,)), ((), ())), preferred_element_type=jnp.float32
        )
        if p == 0:
            back_acc[...] = term
        else:
            back_acc[...] += term

    def write_rows(i, value, target):
        width = target.shape[1]
        parts = value.reshape(EDGE, bricks_dev, EDGE, width)
        for l in range(bricks_dev):
            start = pl.multiple_of(l * brick_rows + i * EDGE * EDGE, EDGE * EDGE)
            piece = parts[:, l].reshape(EDGE * EDGE, width) * act_ref[l].astype(jnp.float32)
            target[pl.ds(start, EDGE * EDGE), :] = piece.astype(jnp.bfloat16)

    def write_forward():
        def one(i, _):
            start = pl.multiple_of(i * plane, plane)
            at = lax.broadcasted_iota(jnp.int32, (EDGE, depth, cout), 1).reshape(plane, cout)
            before = conv_acc[pl.ds(start, plane), 0:cout]
            middle = conv_acc[pl.ds(start, plane), cout : 2 * cout]
            after = conv_acc[pl.ds(start, plane), 2 * cout : 3 * cout]
            value = middle + jnp.where(at == 0, 0.0, pltpu.roll(before, 1, 0))
            value = value + jnp.where(at == depth - 1, 0.0, pltpu.roll(after, plane - 1, 0))
            write_rows(i, value, conv_ref)
            return 0

        lax.fori_loop(0, EDGE, one, 0)

    def write_backward():
        def one(i, _):
            start = pl.multiple_of(i * plane, plane)
            write_rows(i, back_acc[pl.ds(start, plane), :], gfeat_ref)
            return 0

        lax.fori_loop(0, EDGE, one, 0)

    jobs = [functools.partial(backward, p) for p in range(9)] + [write_backward]
    jobs += [functools.partial(forward, p) for p in range(9)] + [write_forward]
    jobs[0:0] = [w_copy.wait]
    jobs[11:11] = [lambda: wait_halo(1)]

    if not fused:
        for p in range(9):
            tap_sums(p)
        for job in jobs:
            job()
        local = pltpu.make_async_copy(ks, gw_hbm, local_sem.at[1])
        local.start()
        local.wait()
    else:
        core, x = lax.rem(s, 2), s // 2
        low, high = lax.rem(b, 2), b // 2
        bits = (core, x, low, high)
        partners = (
            (g, b, s + 1 - 2 * core),
            (g, b, lax.rem(s + 2, m)),
            (g, b + 1 - 2 * low, s),
            (g, lax.rem(b + 2, n), s),
        )
        sizes = [3 * cin >> (level + 1) for level in range(LEVELS)]

        def aligned(value):
            return pl.multiple_of(value, 16)

        bases = [0]
        for level in range(LEVELS):
            bases.append(bases[level] + bits[level] * sizes[level])

        def reduce_copy(p, level):
            if level == 0:
                src = ks.at[p, pl.ds(aligned((1 - core) * sizes[0]), sizes[0])]
            else:
                src = sent[level - 1].at[p]
            return pltpu.make_async_remote_copy(
                src_ref=src, dst_ref=got[level].at[p], send_sem=send.at[p, level], recv_sem=recv.at[p, level],
                device_id=partners[level], device_id_type=MESH,
            )

        def gather_copy(p, level):
            part = out.at[p, pl.ds(aligned(bases[level + 1]), sizes[level])]
            return pltpu.make_async_remote_copy(
                src_ref=part, dst_ref=part, send_sem=send.at[p, LEVELS + level],
                recv_sem=recv.at[p, LEVELS + level], device_id=partners[level], device_id_type=MESH,
            )

        def write_out(p):
            return pltpu.make_async_copy(out.at[p], gw_hbm.at[p], local_sem.at[1 + p])

        def mine(p, level, start, size):
            there = pl.ds(aligned(start), size)
            if level == 0:
                held = ks[p, pl.ds(aligned(core * sizes[0] + start), size)]
            else:
                held = kept[level - 1][p, there]
            return held + got[level][p, there].astype(jnp.float32)

        def stage(k, p):
            if k == 0:
                tap_sums(p)
                reduce_copy(p, 0).start()
            elif k < LEVELS:
                reduce_copy(p, k - 1).wait_recv()
                size = sizes[k]
                sent[k - 1][p] = mine(p, k - 1, (1 - bits[k]) * size, size).astype(WIRE[k])
                reduce_copy(p, k).start()
                kept[k - 1][p] = mine(p, k - 1, bits[k] * size, size)
            elif k == LEVELS:
                reduce_copy(p, k - 1).wait_recv()
                total = mine(p, k - 1, 0, sizes[k - 1])
                out[p, pl.ds(aligned(bases[LEVELS]), sizes[k - 1])] = (total * grad_scale).astype(jnp.bfloat16)
                gather_copy(p, LEVELS - 1).start()
            elif k < 2 * LEVELS:
                gather_copy(p, 2 * LEVELS - k).wait_recv()
                gather_copy(p, 2 * LEVELS - k - 1).start()
            else:
                gather_copy(p, 0).wait_recv()
                write_out(p).start()

        for t in range(9 + STARTS[-1]):
            for k in reversed(range(2 * LEVELS + 1)):
                if 0 <= t - STARTS[k] < 9:
                    stage(k, t - STARTS[k])
            if t >= 1:
                for job in jobs[:PER_STEP]:
                    job()
                jobs = jobs[PER_STEP:]
        for job in jobs:
            job()
        for p in range(9):
            for level in range(LEVELS):
                reduce_copy(p, level).wait_send()
                gather_copy(p, level).wait_send()
            write_out(p).wait()

    for field_at in range(2):
        for side, (db, ds) in enumerate(SIDES):
            @pl.when(inside(db, ds))
            def _():
                halo(field_at, side).wait_send()


def shards(features, active, weight, cotangent):
    n, m = lax.axis_size("bricks"), lax.axis_size("sub")
    bricks_dev = active.shape[0]
    cin, cout = features.shape[1], weight.shape[2]
    rows = features.shape[0]
    depth = bricks_dev * EDGE
    group_rows = 3 * cin
    fused = n == 4 and m == 4 and group_rows % 256 == 0
    sizes = [group_rows >> (level + 1) for level in range(LEVELS)] if fused else [16] * LEVELS
    slots = 2 * LEVELS
    groups = 9 if fused else 1
    grad_scale = 1.0 / math.sqrt(n * m * rows)
    bf16, f32 = jnp.bfloat16, jnp.float32
    vmem = pl.BlockSpec(memory_space=pltpu.VMEM)
    hbm = pl.BlockSpec(memory_space=pltpu.HBM)
    scratch = [
        pltpu.VMEM((rows, cin), bf16),
        pltpu.VMEM((rows, cout), bf16),
        pltpu.VMEM((EDGE + 2, EDGE + 2, depth, cin), bf16),
        pltpu.VMEM((EDGE + 2, EDGE + 2, depth, cout), bf16),
        pltpu.VMEM((EDGE + 2, EDGE + 2, depth, 3 * cout), bf16),
        pltpu.VMEM((cin, rows), bf16),
        pltpu.VMEM(weight.shape, bf16),
        pltpu.VMEM((rows, 3 * cout), f32),
        pltpu.VMEM((rows, cin), f32),
        pltpu.VMEM((9, group_rows, cout), f32),
        pltpu.VMEM((groups, group_rows, cout), bf16),
        [pltpu.VMEM((groups, size, cout), kind) for size, kind in zip(sizes, WIRE)],
        [pltpu.VMEM((groups, size, cout), kind) for size, kind in zip(sizes[1:], WIRE[1:])],
        [pltpu.VMEM((groups, size, cout), f32) for size in sizes[1:]],
        pltpu.SemaphoreType.DMA((2, 8)),
        pltpu.SemaphoreType.DMA((2, 8)),
        pltpu.SemaphoreType.DMA((groups, slots)),
        pltpu.SemaphoreType.DMA((groups, slots)),
        pltpu.SemaphoreType.DMA((12,)),
    ]
    conv_out, grad_features, grad_weight = pl.pallas_call(
        functools.partial(kernel, n, m, fused, grad_scale),
        out_shape=(
            jax.ShapeDtypeStruct((rows, cout), bf16),
            jax.ShapeDtypeStruct((rows, cin), bf16),
            jax.ShapeDtypeStruct((9, group_rows, cout), bf16 if fused else f32),
        ),
        in_specs=[hbm, pl.BlockSpec(memory_space=pltpu.SMEM), hbm, hbm],
        out_specs=(vmem, vmem, pl.BlockSpec(memory_space=pl.ANY)),
        scratch_shapes=scratch,
        compiler_params=pltpu.CompilerParams(
            collective_id=0, has_side_effects=True, vmem_limit_bytes=VMEM_LIMIT
        ),
    )(features, active, weight, cotangent)
    grad_weight = grad_weight.reshape(27, cin, cout)
    if not fused:
        grad_weight = (lax.psum(grad_weight, ("bricks", "sub")) * grad_scale).astype(bf16)
    return (conv_out, grad_features, grad_weight)


def solution(mesh):
    in_specs = (
        P(("groups", "bricks", "sub"), None),
        P(("groups", "bricks", "sub")),
        P(),
        P(("groups", "bricks", "sub"), None),
    )
    out_specs = (
        P(("groups", "bricks", "sub"), None),
        P(("groups", "bricks", "sub"), None),
        P("groups", None, None),
    )
    return jax.shard_map(shards, mesh=mesh, in_specs=in_specs, out_specs=out_specs, check_vma=False)
```
